32 devices in a mesh: groups: 2 (over x), ctx: 16 (over z, y, core).
Axes of the slice: x: 2, y: 2, z: 4, core: 2. Of those that a mesh axis runs over, the one named last changes fastest.
Arguments:
- states: bfloat16 [4096, 3072], P(('groups', 'ctx')), parts along dimension 0, may hold values from -6 to 6
- queries: bfloat16 [4096, 3072], P(('groups', 'ctx')), parts along dimension 0, may hold values from -256 to 256
- keys: bfloat16 [4096, 512], P(('groups', 'ctx')), parts along dimension 0, may hold values from -8 to 8
- values: bfloat16 [4096, 512], P(('groups', 'ctx')), parts along dimension 0, may hold values from -6 to 6
- norm_gain: float32 [3072], replicated, may hold values from 0.5 to 1.5
- router: bfloat16 [3072, 8], replicated, may hold values from -0.109375 to 0.109375
- routes: int32 [4096, 1], P(('groups', 'ctx')), parts along dimension 0, may hold values from 0 to 7; in each aligned block of 128 rows (0 to 127, 128 to 255, ...) at most 18 rows name the same one
- w_gate: bfloat16 [16384, 3072], P('ctx'), may hold values from -0.109375 to 0.109375
- w_up: bfloat16 [16384, 3072], P('ctx'), may hold values from -0.109375 to 0.109375
- w_down: bfloat16 [16384, 3072], P('ctx'), may hold values from -0.0625 to 0.0625
Outputs:
- attended: bfloat16 [4096, 3072], P(('groups', 'ctx')), parts along dimension 0
- mixed_states: bfloat16 [4096, 3072], P(('groups', 'ctx')), parts along dimension 0
The draws below stay inside these ranges and needn't reach their ends.
There are 2 independent parts, one for each index of `groups`. The reference program is written for one: setup_inputs(seed, part) draws one part's arguments, and reference() takes and returns one part's arrays. A program takes and returns all parts, laid end to end along the dimension named above; an argument that names none is the same for every part. Nothing has to cross between parts.
Inputs may be any that keep to these rules, and one draw needn't show every extreme that they name: `routes`: among the rows of one device no expert is named by more than 18 rows, and in every draw some expert is named by exactly 18 rows of some device.
All inputs are finite; a program needn't handle non-finite values.
Results may differ from the reference program's by a relative error of at most 0.004.
Values may be sent and summed in bfloat16 or wider, within the bound.
A program may use at most 320 MiB of HBM per device.

```python
import math
import jax
import jax.numpy as jnp
import numpy as np
from jax import lax

D = 3072
HQ = 24
HK = 4
HD = 128
NEXP = 8
E = 2
FFW = 8192
TOPK = 1
TOK_DEV = 128
CAP = 18
TOKENS = 2048
N_CTX = 16


def shared_keys(key):
    base = jax.random.normal(key, (TOKENS, HK * HD), jnp.float32)
    return base


def draw_keys(key, part):
    drawn = shared_keys(key)
    return jnp.clip(drawn, -7.5, 7.5).astype(jnp.bfloat16)


def draw_queries(key, part):
    key = jax.random.fold_in(key, 5)
    drawn = jax.random.normal(key, (TOKENS, HQ * HD), jnp.float32)
    return jnp.clip(drawn, -250.0, 250.0).astype(jnp.bfloat16)


def block_scale(stream_key, shape, cuts, low, top_value):
    def one(axis_at, blocks):
        steps = jax.random.uniform(jax.random.fold_in(jax.random.fold_in(stream_key, 6), axis_at), (blocks,), jnp.float32, low / len(cuts), top_value / len(cuts))
        return jnp.repeat(jnp.exp(steps), shape[axis_at] // blocks).reshape((-1,) + (1,) * (len(shape) - axis_at - 1))

    level = one(*cuts[0])
    for cut in cuts[1:]:
        level = level * one(*cut)
    return level


def assign_block(own_key, own, number, rows, amount, top, reach, slope):
    order = jax.random.permutation(own_key, amount)
    heavy_load, ordinary = portions_of(amount, rows * top, reach, slope, True), portions_of(amount, rows * top, reach, slope, False)
    places = jnp.arange(amount)

    def named(lengths, rotation):
        used = int((lengths > 0).sum())
        fixed = max(1, used // 4)
        passed = fixed + (places - fixed + rotation * (used - fixed)) % max(1, amount - fixed)
        return jnp.zeros((amount,), jnp.int32).at[order[jnp.where(places < fixed, places, passed)]].set(jnp.asarray(lengths, jnp.int32))

    lengths = jnp.where(number % 4 == 0, named(heavy_load, number // 4), named(ordinary, number - number // 4 - 1))
    mixed = jax.random.permutation(jax.random.fold_in(own, 3), amount)
    source_of, taker = mixed[0:amount // 2 * 2:2], mixed[1:amount // 2 * 2:2]
    margin = jnp.minimum(lengths[source_of] - 1, reach - lengths[taker]) // 2
    margin = jnp.where((source_of == order[0]) | (taker == order[0]) | (lengths[taker] == 0), 0, jnp.maximum(margin, 0))
    passed = jax.random.randint(jax.random.fold_in(own, 4), (amount // 2,), 0, 1 << 20) % (margin + 1)
    lengths = lengths.at[source_of].add(-passed).at[taker].add(passed)
    labels = jnp.searchsorted(jnp.cumsum(lengths), jnp.arange(rows * top), side="right").astype(jnp.int32)
    listing = labels.reshape(top, rows).T
    listing = listing[jax.random.permutation(jax.random.fold_in(own, 1), rows)]
    rotation = jax.random.randint(jax.random.fold_in(own, 2), (rows, 1), 0, top)
    return jnp.take_along_axis(listing, (jnp.arange(top)[None, :] + rotation) % top, axis=1)


def portions_of(amount, total, limit, lean, full):
    portions = [(1 << 20) // math.isqrt(standing ** lean) + 1 for standing in range(1, amount + 1)]
    largest = limit if full else min(limit, max(-(-total // amount), total * portions[0] // sum(portions)))
    least = 1 if total - largest >= amount - 1 else 0
    given, surplus = [largest] + [least] * (amount - 1), total - largest - least * (amount - 1)
    while surplus > 0:
        movable = [i for i in range(1, amount) if given[i] < largest] or [i for i in range(1, amount) if given[i] < limit]
        mass, budget = sum([portions[i] for i in movable]), surplus
        for i in movable:
            more = min(limit - given[i], max(1, budget * portions[i] // mass), surplus)
            given[i] = given[i] + more
            surplus = surplus - more
    return np.array(given)


def bell_draw(rng, extent, spread, reach, split=(), kind=jnp.bfloat16):
    factor_of = block_scale(rng, extent, split, -0.22, 0.18) if split else 1.0
    entries = jax.random.normal(rng, extent, jnp.float32) * spread * factor_of
    return jnp.minimum(jnp.maximum(entries, -reach), reach).astype(kind)


def setup_inputs(seed: int = 0, part: int = 0) -> dict:
    key_list = jax.random.split(jax.random.key(seed), 11)
    part_keys = jax.random.split(jax.random.fold_in(key_list[10], part), 11)
    states = bell_draw(part_keys[0], (TOKENS, D), 1.0, 6.0, ((0, 16),))
    queries = draw_queries(jax.random.fold_in(jax.random.fold_in(key_list[10], part), 71), part)
    keys = draw_keys(jax.random.fold_in(jax.random.fold_in(key_list[10], part), 71), part)
    values = bell_draw(part_keys[3], (TOKENS, HK * HD), 1.0, 6.0, ((0, 16),))
    norm_gain = jnp.clip(1.0 + 0.1 * jax.random.normal(key_list[4], (D,), jnp.float32), 0.5, 1.5)
    router = bell_draw(key_list[5], (D, NEXP), D ** -0.5, 0.109375)
    routes_keys = jax.random.split(jax.random.fold_in(part_keys[6], 1), TOKENS // TOK_DEV)
    routes_turns = jax.random.permutation(jax.random.fold_in(part_keys[6], 3), TOKENS // TOK_DEV)
    routes = jax.vmap(lambda own, number: assign_block(jax.random.fold_in(part_keys[6], 2), own, number, TOK_DEV, NEXP, TOPK, CAP, 2))(routes_keys, routes_turns).reshape((TOKENS, TOPK))
    w_gate = bell_draw(key_list[7], (E * FFW, D), D ** -0.5, 0.109375, ((0, 16),))
    w_up = bell_draw(key_list[8], (E * FFW, D), D ** -0.5, 0.109375, ((0, 16),))
    w_down = bell_draw(key_list[9], (E * FFW, D), FFW ** -0.5, 0.0625, ((0, 16),))
    return dict(states=states, queries=queries, keys=keys, values=values, norm_gain=norm_gain, router=router, routes=routes, w_gate=w_gate, w_up=w_up, w_down=w_down)


def expert_slice(rows, gate_rows, up_rows, down_rows):
    dims = (((1,), (1,)), ((), ()))
    gated = lax.dot_general(rows, gate_rows, dims, preferred_element_type=jnp.float32)
    upward = lax.dot_general(rows, up_rows, dims, preferred_element_type=jnp.float32)
    hidden = (jax.nn.silu(gated) * upward).astype(jnp.bfloat16)
    return jnp.dot(hidden, down_rows, preferred_element_type=jnp.float32)

def reference(states, queries, keys, values, norm_gain, router, routes, w_gate, w_up, w_down):
    seq_rows = states.shape[0]
    group = HQ // HK
    key_grid = keys.astype(jnp.float32).reshape(seq_rows, HK, HD)
    value_grid = values.astype(jnp.float32).reshape(seq_rows, HK, HD)
    block = math.gcd(seq_rows, 512)
    key_positions = jnp.arange(seq_rows, dtype=jnp.int32)

    def attend(start):
        query_block = lax.dynamic_slice_in_dim(queries, start, block, 0).astype(jnp.float32).reshape(block, HK, group, HD)
        scores = jnp.einsum('qhgd,khd->hgqk', query_block, key_grid) / math.sqrt(HD)
        query_positions = start + jnp.arange(block, dtype=jnp.int32)
        visible = key_positions[None, :] <= query_positions[:, None]
        scores = jnp.where(visible, scores, -1e+30)
        highest = lax.optimization_barrier(jnp.max(scores, axis=-1, keepdims=True))
        expo = jnp.where(visible, jnp.exp(scores - highest), 0.0)
        totals = lax.optimization_barrier(jnp.sum(expo, axis=-1))
        probs = lax.optimization_barrier(expo.astype(jnp.bfloat16)).astype(jnp.float32)
        result = jnp.einsum('hgqk,khd->hgqd', probs, value_grid) / totals[..., None]
        return result.transpose(2, 0, 1, 3).reshape(block, HQ * HD).astype(jnp.bfloat16)
    starts = jnp.arange(0, seq_rows, block, dtype=jnp.int32)
    attended = lax.map(attend, starts).reshape(seq_rows, HQ * HD)
    wide = states.astype(jnp.float32)
    meansq = lax.optimization_barrier(jnp.mean(wide * wide, axis=-1, keepdims=True))
    normed = (wide * lax.rsqrt(meansq + 1e-05) * norm_gain).astype(jnp.bfloat16)
    logits = jnp.dot(normed, router, preferred_element_type=jnp.float32)
    chosen = routes[:, 0]
    picked = jnp.take_along_axis(logits, routes, axis=1)[:, 0]
    mixing = jax.nn.sigmoid(picked)
    slices = N_CTX // E
    part = FFW // slices
    bound = min(seq_rows, CAP * N_CTX)
    expert_out = jnp.zeros((seq_rows, D), jnp.float32)
    for expert in range(E):
        member = chosen == expert
        ordering = jnp.argsort(jnp.where(member, 0, 1).astype(jnp.int32), stable=True)[:bound].astype(jnp.int32)
        rows = jnp.take(normed, ordering, axis=0)
        valid = jnp.take(member, ordering)
        weights = jnp.take(mixing, ordering)
        total = jnp.zeros((bound, D), jnp.float32)
        for piece in range(slices):
            low = expert * FFW + piece * part
            partial_value = expert_slice(rows, w_gate[low:low + part], w_up[low:low + part], w_down[low:low + part])
            total = total + lax.optimization_barrier(partial_value.astype(jnp.bfloat16)).astype(jnp.float32)
        expert_out = expert_out.at[ordering].add(jnp.where(valid[:, None], weights[:, None] * total, 0.0))
    return (attended, (wide + expert_out).astype(jnp.bfloat16))
```

```python
import functools
import math

import jax
import jax.numpy as jnp
from jax import lax
from jax.experimental import pallas as pl
from jax.experimental.pallas import tpu as pltpu
from jax.sharding import PartitionSpec as P

HD = 128
E = 2
CAP = 18
MAIN = 16
Q = 4
MESH = pl.DeviceIdType.MESH
F32 = jnp.float32
BF16 = jnp.bfloat16
NT = (((1,), (1,)), ((), ()))


def iota(shape, dim):
    return lax.broadcasted_iota(jnp.int32, shape, dim)


def onehot(mask):
    return jnp.where(mask, 1.0, 0.0).astype(BF16)


def kernel(n, states, queries, keys, values, gain, router, routes, w_gate, w_up, w_down,
           attended, mixed, kv, x, x2, xb, part, hid, wg, wu, wd, r1, r2, r3, qs, m_sc, l_sc, acc,
           w_sem, loc_sem, kv_send, kv_recv, x_send, x_recv, r_send, r_recv, z_send, z_recv):
    rows, width = states.shape
    lines = n // Q
    per = lines // E
    kvw = keys.shape[1]
    heads = kvw // HD
    group = queries.shape[1] // kvw
    pack = width // 8
    wide = width + pack
    me = lax.axis_index("ctx")
    z = me // Q
    y = (me % Q) // 2
    c = me % 2
    ymate = z * Q + (1 - y) * 2 + c
    cmate = z * Q + y * 2 + (1 - c)

    def dev(zz, yy, cc):
        return zz * Q + yy * 2 + cc

    def slot(p):
        return ((p % 2) * 2 + (p % Q) // 2) * lines + p // Q

    def wcopy(i):
        src = (w_gate, w_up, w_down)[i]
        dst = (wg, wu, wd)[i]
        return pltpu.make_async_copy(src, dst, w_sem.at[i])

    def own_kv(i):
        src = (keys, values)[i]
        return pltpu.make_async_copy(
            src, kv.at[pl.ds(pl.multiple_of(me * rows, rows), rows), pl.ds(i * kvw, kvw)], loc_sem.at[i])

    own_kv(0).start()
    own_kv(1).start()
    for i in range(3):
        wcopy(i).start()

    barrier = pltpu.get_barrier_semaphore()
    for d in range(1, lines):
        pl.semaphore_signal(barrier, inc=1, device_id={"ctx": dev((z + d) % lines, y, c)}, device_id_type=MESH)
    for mate in (ymate, cmate):
        pl.semaphore_signal(barrier, inc=1, device_id={"ctx": mate}, device_id_type=MESH)

    def kv_block(p):
        return kv.at[pl.ds(pl.multiple_of(p * rows, rows), rows)]

    def kv_copy(kind, index, p, to):
        return pltpu.make_async_remote_copy(
            src_ref=kv_block(p), dst_ref=kv_block(p), send_sem=kv_send.at[kind, index], recv_sem=kv_recv.at[p],
            device_id={"ctx": to}, device_id_type=MESH)

    def x_block(p):
        return x.at[pl.ds(pl.multiple_of(slot(p) * MAIN, MAIN), MAIN)]

    def x_copy(kind, index, p, to):
        return pltpu.make_async_remote_copy(
            src_ref=x_block(p), dst_ref=x_block(p), send_sem=x_send.at[kind, index], recv_sem=x_recv.at[p],
            device_id={"ctx": to}, device_id_type=MESH)

    def x_line(zt):
        return pltpu.make_async_remote_copy(
            src_ref=xb.at[pl.ds((zt // per) * MAIN, MAIN)], dst_ref=x_block(me), send_sem=x_send.at[0, zt],
            recv_sem=x_recv.at[me], device_id={"ctx": dev(zt, y, c)}, device_id_type=MESH)

    st = states[...].astype(F32)
    meansq = jnp.mean(st * st, axis=-1, keepdims=True)
    normed = (st * lax.rsqrt(meansq + 1e-05) * gain[...]).astype(BF16)
    chosen = routes[...]
    member = chosen == iota((rows, HD), 1)
    before = onehot(iota((rows, rows), 1) < iota((rows, rows), 0))
    ahead = jnp.dot(before, onehot(member), preferred_element_type=F32)
    rank = jnp.sum(jnp.where(member, ahead, 0.0), axis=1, keepdims=True).astype(jnp.int32)
    lane = iota((rows, HD), 1)
    main_slot = jnp.where((chosen < E) & (rank < MAIN), chosen * MAIN + rank, -1)
    place = jnp.transpose(jnp.where(main_slot == lane, 1.0, 0.0)).astype(BF16)[: E * MAIN]
    xb[:, :width] = jnp.dot(place, normed, preferred_element_type=F32).astype(BF16)
    ext_slot = jnp.where((chosen < E) & (rank >= MAIN), chosen * MAIN + (rank - MAIN) * 8, -HD)
    ext = jnp.zeros((E * MAIN, pack), F32)
    for k in range(8):
        sel = jnp.transpose(jnp.where(ext_slot + k == lane, 1.0, 0.0)).astype(BF16)[: E * MAIN]
        ext += jnp.dot(sel, normed[:, k * pack:(k + 1) * pack], preferred_element_type=F32)
    xb[:, width:] = ext.astype(BF16)
    logits = jnp.dot(normed, router[...], preferred_element_type=F32)
    picked = jnp.sum(jnp.where(chosen == iota(logits.shape, 1), logits, 0.0), axis=1, keepdims=True)
    mixing = jax.nn.sigmoid(picked)

    x[pl.ds(pl.multiple_of(slot(me) * MAIN, MAIN), MAIN), :] = jnp.where(z < per, xb[:MAIN, :], xb[MAIN:, :])

    pl.semaphore_wait(barrier, lines + 1)

    for zt in range(lines):
        @pl.when(zt != z)
        def _(zt=zt):
            x_line(zt).start()

    def x_forward(d):
        zs = (z + d) % lines
        p = dev(zs, y, c)
        if d:
            x_copy(0, 0, p, me).wait_recv()
        x_copy(1, d, p, ymate).start()
        x_copy(2, d, p, cmate).start()

    def x_forward_y(d):
        zs = (z + d) % lines
        p = dev(zs, 1 - y, c)
        x_copy(1, d, p, ymate).wait_recv()
        x_copy(3, d, p, cmate).start()

    def x_wait(d):
        zs = (z + d) % lines
        x_copy(2, d, dev(zs, y, 1 - c), cmate).wait_recv()
        x_copy(3, d, dev(zs, 1 - y, 1 - c), cmate).wait_recv()

    def kv_line(d):
        return kv_copy(0, d, me, dev(z + d, y, c))

    def kv_forward(d):
        p = dev(z - d, y, c)

        @pl.when(z >= d)
        def _():
            if d:
                kv_copy(0, d, p, me).wait_recv()
            kv_copy(1, d, p, ymate).start()
            kv_copy(2, d, p, cmate).start()

    def kv_forward_y(d):
        p = dev(z - d, 1 - y, c)

        @pl.when(z >= d)
        def _():
            kv_copy(1, d, p, ymate).wait_recv()
            kv_copy(3, d, p, cmate).start()

    def kv_wait(d):
        @pl.when(z >= d)
        def _():
            kv_copy(2, d, dev(z - d, y, 1 - c), cmate).wait_recv()
            kv_copy(3, d, dev(z - d, 1 - y, 1 - c), cmate).wait_recv()

    x_forward(0)
    own_kv(0).wait()
    own_kv(1).wait()
    for d in range(1, lines):
        @pl.when(z + d < lines)
        def _(d=d):
            kv_line(d).start()
    kv_forward(0)

    for h in range(heads * group):
        qs[h * rows:(h + 1) * rows, :] = queries[:, h * HD:(h + 1) * HD]

    block = group * rows
    span = Q * rows
    scale = math.log2(math.e) / math.sqrt(HD)

    def attend(zs, masked):
        def head(h, carry):
            at = pl.ds(pl.multiple_of(h * block, block), block)
            keys_at = pl.ds(pl.multiple_of(zs * span, span), span)
            k = kv[keys_at, pl.ds(pl.multiple_of(h * HD, HD), HD)]
            v = kv[keys_at, pl.ds(pl.multiple_of(kvw + h * HD, HD), HD)]
            s = lax.dot_general(qs[at, :], k, NT, preferred_element_type=F32) * scale
            if masked:
                seen = iota((block, span), 1) <= (me % Q) * rows + iota((block, span), 0) % rows
                s = jnp.where(seen, s, -1e30)
            top = jnp.max(s, axis=-1, keepdims=True)
            if not masked:
                old = m_sc[at, :1]
                top = jnp.maximum(old, top)
            e = jnp.exp2(s - top)
            total = jnp.sum(e, axis=-1, keepdims=True)
            out = jnp.dot(e.astype(BF16), v, preferred_element_type=F32)
            if not masked:
                fade = jnp.exp2(old - top)
                total += fade * l_sc[at, :1]
                out += fade * acc[at, :]
            m_sc[at, :] = jnp.broadcast_to(top, (block, HD))
            l_sc[at, :] = jnp.broadcast_to(total, (block, HD))
            acc[at, :] = out
            return carry

        lax.fori_loop(0, heads, head, 0)

    for d in range(1, lines):
        x_forward(d)
    for d in range(lines):
        x_forward_y(d)
    kv_forward_y(0)
    for d in range(lines):
        x_wait(d)

    slots = n * MAIN
    over = 2 * n

    def unpick(k, shape, s_dim):
        j, i = iota(shape, 1 - s_dim), iota(shape, s_dim)
        return onehot((i // MAIN == j // 2) & (i % MAIN == (j % 2) * 8 + k))

    x2[:slots, :] = x[:, :width]
    for k in range(8):
        x2[slots:, k * pack:(k + 1) * pack] = jnp.dot(
            unpick(k, (over, slots), 1), x[:, width:], preferred_element_type=F32).astype(BF16)

    units = w_gate.shape[0]
    chunk = min(256, units)
    wcopy(0).wait()
    wcopy(1).wait()
    steps = units // chunk

    def gate_up(i, carry):
        at = pl.ds(pl.multiple_of(i * chunk, chunk), chunk)
        g = lax.dot_general(x2[...], wg[at, :], NT, preferred_element_type=F32)
        u = lax.dot_general(x2[...], wu[at, :], NT, preferred_element_type=F32)
        hid[:, at] = (g / (1.0 + jnp.exp(-g)) * u).astype(BF16)
        return carry

    lax.fori_loop(0, steps // 2, gate_up, 0)
    if lines > 1:
        kv_forward(1)
    lax.fori_loop(steps // 2, steps, gate_up, 0)
    if lines > 1:
        kv_forward_y(1)
    if lines > 2:
        kv_forward(2)
    wcopy(2).wait()

    part[:, width:] = jnp.zeros((slots, pack), BF16)

    def down(i, carry):
        at = pl.ds(pl.multiple_of(i * 2 * pack, 2 * pack), 2 * pack)
        o = jnp.dot(hid[...], wd[:, at], preferred_element_type=F32).astype(BF16)
        part[:, at] = o[:slots]
        for k in range(2):
            part[:, width:] += jnp.dot(
                unpick(2 * i + k, (slots, over), 0), o[slots:, k * pack:(k + 1) * pack],
                preferred_element_type=F32).astype(BF16)
        return carry

    lax.fori_loop(0, 4, down, 0)

    half, quart = slots // 2, slots // 4

    def core_swap():
        return pltpu.make_async_remote_copy(
            src_ref=part.at[pl.ds(pl.multiple_of((1 - c) * half, half), half)], dst_ref=r1,
            send_sem=r_send.at[0], recv_sem=r_recv.at[0], device_id={"ctx": cmate}, device_id_type=MESH)

    def y_swap():
        return pltpu.make_async_remote_copy(
            src_ref=part.at[pl.ds(pl.multiple_of((c * 2 + 1 - y) * quart, quart), quart)], dst_ref=r2,
            send_sem=r_send.at[1], recv_sem=r_recv.at[1], device_id={"ctx": ymate}, device_id_type=MESH)

    def line_back(zt, at):
        return pltpu.make_async_remote_copy(
            src_ref=part.at[pl.ds(pl.multiple_of((c * 2 + y) * quart + zt * MAIN, MAIN), MAIN)], dst_ref=r3.at[pl.ds(pl.multiple_of(at * MAIN, MAIN), MAIN)],
            send_sem=z_send.at[zt], recv_sem=z_recv.at[at], device_id={"ctx": dev(zt, y, c)}, device_id_type=MESH)

    core_swap().start()
    kv_wait(0)
    attend(z, True)
    for d in range(3, lines):
        kv_forward(d)
    for d in range(2, lines):
        kv_forward_y(d)

    core_swap().wait_recv()
    mine = pl.ds(pl.multiple_of(c * half, half), half)
    part[mine, :] = (part[mine, :].astype(F32) + r1[...].astype(F32)).astype(BF16)
    y_swap().start()
    if lines > 1:
        kv_wait(1)

        @pl.when(z >= 1)
        def _():
            attend(z - 1, False)

    y_swap().wait_recv()
    mine = pl.ds(pl.multiple_of((c * 2 + y) * quart, quart), quart)
    part[mine, :] = (part[mine, :].astype(F32) + r2[...].astype(F32)).astype(BF16)
    for zt in range(lines):
        @pl.when(zt != z)
        def _(zt=zt):
            line_back(zt, z).start()

        @pl.when(zt == z)
        def _(zt=zt):
            r3[zt * MAIN:(zt + 1) * MAIN, :] = part[pl.ds(pl.multiple_of((c * 2 + y) * quart + zt * MAIN, MAIN), MAIN), :]

    for d in range(2, lines):
        kv_wait(d)

    def far(d, carry):
        attend(z - d, False)
        return carry

    lax.fori_loop(2, z + 1, far, 0)

    def write(h, carry):
        at = pl.ds(pl.multiple_of(h * block, block), block)
        o = (acc[at, :] / l_sc[at, :]).astype(BF16)
        for g in range(group):
            attended[:, pl.ds(pl.multiple_of(h * block + g * HD, HD), HD)] = o[g * rows:(g + 1) * rows, :]
        return carry

    lax.fori_loop(0, heads, write, 0)

    for zs in range(lines):
        @pl.when(zs != z)
        def _(zs=zs):
            line_back(zs, zs).wait_recv()

    col = iota((rows, lines * MAIN), 1)
    owns = chosen == col // (per * MAIN)
    pick_main = onehot(owns & (rank == col % MAIN))
    for k in range(8):
        at = slice(k * pack, (k + 1) * pack)
        pick_ext = onehot(owns & (rank >= MAIN) & ((rank - MAIN) * 8 + k == col % MAIN))
        sums = jnp.dot(pick_main, r3[:, at], preferred_element_type=F32)
        sums += jnp.dot(pick_ext, r3[:, width:], preferred_element_type=F32)
        mixed[:, at] = (states[:, at].astype(F32) + mixing * sums).astype(BF16)

    core_swap().wait_send()
    y_swap().wait_send()
    for zt in range(lines):
        @pl.when(zt != z)
        def _(zt=zt):
            line_back(zt, z).wait_send()
            x_line(zt).wait_send()
    for d in range(lines):
        p = dev((z + d) % lines, y, c)
        x_copy(1, d, p, ymate).wait_send()
        x_copy(2, d, p, cmate).wait_send()
        x_copy(3, d, dev((z + d) % lines, 1 - y, c), cmate).wait_send()

        @pl.when(z >= d)
        def _(d=d):
            kv_copy(1, d, dev(z - d, y, c), ymate).wait_send()
            kv_copy(2, d, dev(z - d, y, c), cmate).wait_send()
            kv_copy(3, d, dev(z - d, 1 - y, c), cmate).wait_send()
        if d:
            @pl.when(z + d < lines)
            def _(d=d):
                kv_line(d).wait_send()


def solution(mesh):
    n = mesh.shape["ctx"]
    lines = n // Q

    def body(states, queries, keys, values, norm_gain, router, routes, w_gate, w_up, w_down):
        rows, width = states.shape
        kvw = keys.shape[1]
        units = w_gate.shape[0]
        qrows = rows * queries.shape[1] // HD
        slots = n * MAIN
        wide = width + width // 8
        vm = pl.BlockSpec(memory_space=pltpu.VMEM)
        hb = pl.BlockSpec(memory_space=pl.ANY)
        dma = pltpu.SemaphoreType.DMA
        return pl.pallas_call(
            functools.partial(kernel, n),
            out_shape=(jax.ShapeDtypeStruct(queries.shape, BF16), jax.ShapeDtypeStruct(states.shape, BF16)),
            in_specs=[vm, vm, hb, hb, vm, vm, vm, hb, hb, hb],
            out_specs=(vm, vm),
            scratch_shapes=[
                pltpu.VMEM((n * rows, 2 * kvw), BF16),
                pltpu.VMEM((slots, wide), BF16),
                pltpu.VMEM((slots + 2 * n, width), BF16),
                pltpu.VMEM((E * MAIN, wide), BF16),
                pltpu.VMEM((slots, wide), BF16),
                pltpu.VMEM((slots + 2 * n, units), BF16),
                pltpu.VMEM((units, width), BF16),
                pltpu.VMEM((units, width), BF16),
                pltpu.VMEM((units, width), BF16),
                pltpu.VMEM((slots // 2, wide), BF16),
                pltpu.VMEM((slots // 4, wide), BF16),
                pltpu.VMEM((lines * MAIN, wide), BF16),
                pltpu.VMEM((qrows, HD), BF16),
                pltpu.VMEM((qrows, HD), F32),
                pltpu.VMEM((qrows, HD), F32),
                pltpu.VMEM((qrows, HD), F32),
                dma((3,)),
                dma((2,)),
                dma((4, lines)),
                dma((n,)),
                dma((4, lines)),
                dma((n,)),
                dma((2,)),
                dma((2,)),
                dma((lines,)),
                dma((lines,)),
            ],
            compiler_params=pltpu.CompilerParams(
                collective_id=0, has_side_effects=True, vmem_limit_bytes=63 * 1024 * 1024),
        )(states, queries, keys, values, norm_gain.reshape(1, width), router, routes, w_gate, w_up, w_down)

    tokens = P(("groups", "ctx"), None)
    units = P("ctx", None)
    return jax.shard_map(
        body, mesh=mesh,
        in_specs=(tokens, tokens, tokens, tokens, P(), P(), tokens, units, units, units),
        out_specs=(tokens, tokens), check_vma=False)
```

```python
import functools
import math

import jax
import jax.numpy as jnp
from jax import lax
from jax.experimental import pallas as pl
from jax.experimental.pallas import tpu as pltpu
from jax.sharding import PartitionSpec as P

HD = 128
E = 2
CAP = 18
MAIN = 16
Q = 4
MESH = pl.DeviceIdType.MESH
F32 = jnp.float32
BF16 = jnp.bfloat16
NT = (((1,), (1,)), ((), ()))


def iota(shape, dim):
    return lax.broadcasted_iota(jnp.int32, shape, dim)


def onehot(mask):
    return jnp.where(mask, 1.0, 0.0).astype(BF16)


def kernel(n, states, queries, keys, values, gain, router, routes, w_gate, w_up, w_down,
           attended, mixed, kv, x, x2, xb, part, hid, wg, wu, wd, r1, r2, r3, qs, m_sc, l_sc, acc,
           w_sem, loc_sem, kv_send, kv_recv, x_send, x_recv, r_send, r_recv, z_send, z_recv):
    rows, width = states.shape
    lines = n // Q
    per = lines // E
    kvw = keys.shape[1]
    heads = kvw // HD
    group = queries.shape[1] // kvw
    pack = width // 8
    wide = width + pack
    me = lax.axis_index("ctx")
    z = me // Q
    y = (me % Q) // 2
    c = me % 2
    ymate = z * Q + (1 - y) * 2 + c
    cmate = z * Q + y * 2 + (1 - c)

    def dev(zz, yy, cc):
        return zz * Q + yy * 2 + cc

    def slot(p):
        return ((p % 2) * 2 + (p % Q) // 2) * lines + p // Q

    def wcopy(i):
        src = (w_gate, w_up, w_down)[i]
        dst = (wg, wu, wd)[i]
        return pltpu.make_async_copy(src, dst, w_sem.at[i])

    def own_kv(i):
        src = (keys, values)[i]
        return pltpu.make_async_copy(
            src, kv.at[pl.ds(pl.multiple_of(me * rows, rows), rows), pl.ds(i * kvw, kvw)], loc_sem.at[i])

    own_kv(0).start()
    own_kv(1).start()
    for i in range(3):
        wcopy(i).start()

    barrier = pltpu.get_barrier_semaphore()
    for d in range(1, lines):
        pl.semaphore_signal(barrier, inc=1, device_id={"ctx": dev((z + d) % lines, y, c)}, device_id_type=MESH)
    for mate in (ymate, cmate):
        pl.semaphore_signal(barrier, inc=1, device_id={"ctx": mate}, device_id_type=MESH)

    def kv_block(p):
        return kv.at[pl.ds(pl.multiple_of(p * rows, rows), rows)]

    def kv_copy(kind, index, p, to):
        return pltpu.make_async_remote_copy(
            src_ref=kv_block(p), dst_ref=kv_block(p), send_sem=kv_send.at[kind, index], recv_sem=kv_recv.at[p],
            device_id={"ctx": to}, device_id_type=MESH)

    def x_block(p):
        return x.at[pl.ds(pl.multiple_of(slot(p) * MAIN, MAIN), MAIN)]

    def x_copy(kind, index, p, to):
        return pltpu.make_async_remote_copy(
            src_ref=x_block(p), dst_ref=x_block(p), send_sem=x_send.at[kind, index], recv_sem=x_recv.at[p],
            device_id={"ctx": to}, device_id_type=MESH)

    def x_line(zt):
        return pltpu.make_async_remote_copy(
            src_ref=xb.at[pl.ds((zt // per) * MAIN, MAIN)], dst_ref=x_block(me), send_sem=x_send.at[0, zt],
            recv_sem=x_recv.at[me], device_id={"ctx": dev(zt, y, c)}, device_id_type=MESH)

    def kv_line(d):
        return kv_copy(0, d, me, dev(z + d, y, c))

    def kv_forward(d):
        p = dev(z - d, y, c)

        @pl.when(z >= d)
        def _():
            if d:
                kv_copy(0, d, p, me).wait_recv()
            kv_copy(1, d, p, ymate).start()
            kv_copy(2, d, p, cmate).start()

    def kv_forward_y(d):
        p = dev(z - d, 1 - y, c)

        @pl.when(z >= d)
        def _():
            kv_copy(1, d, p, ymate).wait_recv()
            kv_copy(3, d, p, cmate).start()

    def kv_wait(d):
        @pl.when(z >= d)
        def _():
            kv_copy(2, d, dev(z - d, y, 1 - c), cmate).wait_recv()
            kv_copy(3, d, dev(z - d, 1 - y, 1 - c), cmate).wait_recv()

    own_kv(0).wait()
    own_kv(1).wait()
    pl.semaphore_wait(barrier, lines + 1)
    kv_forward(0)

    st = states[...].astype(F32)
    meansq = jnp.mean(st * st, axis=-1, keepdims=True)
    normed = (st * lax.rsqrt(meansq + 1e-05) * gain[...]).astype(BF16)
    chosen = jnp.transpose(jnp.broadcast_to(routes[...].astype(F32), (HD, rows)))[:, :1].astype(jnp.int32)
    member = chosen == iota((rows, HD), 1)
    before = onehot(iota((rows, rows), 1) < iota((rows, rows), 0))
    ahead = jnp.dot(before, onehot(member), preferred_element_type=F32)
    rank = jnp.sum(jnp.where(member, ahead, 0.0), axis=1, keepdims=True).astype(jnp.int32)
    down_rows = iota((E * MAIN, rows), 0)

    def across(v):
        return jnp.transpose(jnp.broadcast_to(v.astype(F32), (rows, HD)))[: E * MAIN].astype(jnp.int32)

    main_slot = jnp.where((chosen < E) & (rank < MAIN), chosen * MAIN + rank, -1)
    place = onehot(across(main_slot) == down_rows)
    xb[:, :width] = jnp.dot(place, normed, preferred_element_type=F32).astype(BF16)
    ext_slot = jnp.where((chosen < E) & (rank >= MAIN), chosen * MAIN + (rank - MAIN) * 8, -HD)
    ext_slot = across(ext_slot)
    ext = jnp.zeros((E * MAIN, pack), F32)
    for k in range(8):
        sel = onehot(ext_slot + k == down_rows)
        ext += jnp.dot(sel, normed[:, k * pack:(k + 1) * pack], preferred_element_type=F32)
    xb[:, width:] = ext.astype(BF16)
    logits = lax.dot_general(normed, router[...], NT, preferred_element_type=F32)
    picked = jnp.sum(jnp.where(chosen == iota(logits.shape, 1), logits, 0.0), axis=1, keepdims=True)
    mixing = jax.nn.sigmoid(picked)

    x[pl.ds(pl.multiple_of(slot(me) * MAIN, MAIN), MAIN), :] = jnp.where(z < per, xb[:MAIN, :], xb[MAIN:, :])

    for zt in range(lines):
        @pl.when(zt != z)
        def _(zt=zt):
            x_line(zt).start()

    def x_forward(d):
        zs = (z + d) % lines
        p = dev(zs, y, c)
        if d:
            x_copy(0, 0, p, me).wait_recv()
        x_copy(1, d, p, ymate).start()
        x_copy(2, d, p, cmate).start()

    def x_forward_y(d):
        zs = (z + d) % lines
        p = dev(zs, 1 - y, c)
        x_copy(1, d, p, ymate).wait_recv()
        x_copy(3, d, p, cmate).start()

    def x_wait(d):
        zs = (z + d) % lines
        x_copy(2, d, dev(zs, y, 1 - c), cmate).wait_recv()
        x_copy(3, d, dev(zs, 1 - y, 1 - c), cmate).wait_recv()

    x_forward(0)
    for d in range(1, lines):
        @pl.when(z + d < lines)
        def _(d=d):
            kv_line(d).start()
    for h in range(heads * group):
        qs[h * rows:(h + 1) * rows, :] = queries[:, h * HD:(h + 1) * HD]

    block = group * rows
    span = Q * rows
    scale = math.log2(math.e) / math.sqrt(HD)

    tile = block // 2

    def attend(zs, masked, first=0, last=heads):
        def head(h, carry):
            keys_at = pl.ds(pl.multiple_of(zs * span, span), span)
            k = kv[keys_at, pl.ds(pl.multiple_of(h * HD, HD), HD)]
            v = kv[keys_at, pl.ds(pl.multiple_of(kvw + h * HD, HD), HD)]
            both = jnp.concatenate([v, jnp.ones((span, HD), BF16)], axis=1)
            for low in range(0, block, tile):
                at = pl.ds(pl.multiple_of(h * block + low, tile), tile)
                s = lax.dot_general(qs[at, :], k, NT, preferred_element_type=F32) * scale
                if masked:
                    seen = iota((tile, span), 1) <= (me % Q) * rows + iota((tile, span), 0) % rows
                    s = jnp.where(seen, s, -1e30)
                top = jnp.max(s, axis=-1, keepdims=True)
                if not masked:
                    old = m_sc[at, :1]
                    top = jnp.maximum(old, top)
                e = jnp.exp2(s - top).astype(BF16)
                sums = jnp.dot(e, both, preferred_element_type=F32)
                out, total = sums[:, :HD], sums[:, HD:]
                if not masked:
                    fade = jnp.exp2(old - top)
                    total += fade * l_sc[at, :]
                    out += fade * acc[at, :]
                m_sc[at, :] = jnp.broadcast_to(top, (tile, HD))
                l_sc[at, :] = total
                acc[at, :] = out
            return carry

        lax.fori_loop(first, last, head, 0)

    kv_forward_y(0)
    kv_wait(0)
    for h in range(heads):
        attend(z, True, h, h + 1)
        for d in range(1, lines):
            if (d - 1) * heads // (lines - 1) == h:
                x_forward(d)
    for d in range(lines):
        x_forward_y(d)
    for d in range(lines):
        x_wait(d)

    slots = n * MAIN
    over = 2 * n

    def unpick(k, shape, s_dim):
        j, i = iota(shape, 1 - s_dim), iota(shape, s_dim)
        return onehot((i // MAIN == j // 2) & (i % MAIN == (j % 2) * 8 + k))

    x2[:slots, :] = x[:, :width]
    for k in range(8):
        x2[slots:, k * pack:(k + 1) * pack] = jnp.dot(
            unpick(k, (over, slots), 1), x[:, width:], preferred_element_type=F32).astype(BF16)

    units = w_gate.shape[0]
    chunk = min(256, units)
    wcopy(0).wait()
    wcopy(1).wait()
    steps = units // chunk

    def gate_up(i, carry):
        at = pl.ds(pl.multiple_of(i * chunk, chunk), chunk)
        g = lax.dot_general(x2[...], wg[at, :], NT, preferred_element_type=F32)
        u = lax.dot_general(x2[...], wu[at, :], NT, preferred_element_type=F32)
        hid[:, at] = (g / (1.0 + jnp.exp(-g)) * u).astype(BF16)
        return carry

    lax.fori_loop(0, steps // 2, gate_up, 0)
    if lines > 1:
        kv_forward(1)
    lax.fori_loop(steps // 2, steps, gate_up, 0)
    if lines > 1:
        kv_forward_y(1)
    if lines > 2:
        kv_forward(2)
    wcopy(2).wait()

    part[:, width:] = jnp.zeros((slots, pack), BF16)

    def down(i, carry):
        at = pl.ds(pl.multiple_of(i * 2 * pack, 2 * pack), 2 * pack)
        o = jnp.dot(hid[...], wd[:, at], preferred_element_type=F32).astype(BF16)
        part[:, at] = o[:slots]
        for k in range(2):
            part[:, width:] += jnp.dot(
                unpick(2 * i + k, (slots, over), 0), o[slots:, k * pack:(k + 1) * pack],
                preferred_element_type=F32).astype(BF16)
        return carry

    half, quart = slots // 2, slots // 4
    sides = ((0, 4 * pack), (4 * pack, wide - 4 * pack))

    def swap(src_at, dst, k, i, to):
        cols = pl.ds(*sides[i])
        return pltpu.make_async_remote_copy(
            src_ref=part.at[src_at, cols], dst_ref=dst.at[:, cols], send_sem=r_send.at[k, i],
            recv_sem=r_recv.at[k, i], device_id={"ctx": to}, device_id_type=MESH)

    def core_swap(i):
        return swap(pl.ds(pl.multiple_of((1 - c) * half, half), half), r1, 0, i, cmate)

    def y_swap(i):
        return swap(pl.ds(pl.multiple_of((c * 2 + 1 - y) * quart, quart), quart), r2, 1, i, ymate)

    def own_rows(zt):
        return pl.ds(pl.multiple_of((c * 2 + y) * quart + zt * MAIN, MAIN), MAIN)

    def line_back(i, zt, at):
        cols = pl.ds(*sides[i])
        return pltpu.make_async_remote_copy(
            src_ref=part.at[own_rows(zt), cols],
            dst_ref=r3.at[pl.ds(pl.multiple_of(at * MAIN, MAIN), MAIN), cols],
            send_sem=z_send.at[i, zt], recv_sem=z_recv.at[i, at], device_id={"ctx": dev(zt, y, c)},
            device_id_type=MESH)

    def add(at, other, i):
        cols = pl.ds(*sides[i])
        part[at, cols] = (part[at, cols].astype(F32) + other[:, cols].astype(F32)).astype(BF16)

    def after_core(i):
        core_swap(i).wait_recv()
        add(pl.ds(pl.multiple_of(c * half, half), half), r1, i)
        y_swap(i).start()

    def after_y(i):
        y_swap(i).wait_recv()
        add(pl.ds(pl.multiple_of((c * 2 + y) * quart, quart), quart), r2, i)
        cols = pl.ds(*sides[i])
        for zt in range(lines):
            @pl.when(zt != z)
            def _(zt=zt):
                line_back(i, zt, z).start()

            @pl.when(zt == z)
            def _(zt=zt):
                r3[zt * MAIN:(zt + 1) * MAIN, cols] = part[own_rows(zt), cols]

    def attend_back(d, first, last):
        if d < lines:
            @pl.when(z >= d)
            def _():
                attend(z - d, False, first, last)

    lax.fori_loop(0, 2, down, 0)
    core_swap(0).start()
    lax.fori_loop(2, 4, down, 0)
    core_swap(1).start()
    for d in range(3, lines):
        kv_forward(d)
    for d in range(2, lines):
        kv_forward_y(d)
    after_core(0)
    if lines > 1:
        kv_wait(1)
    attend_back(1, 0, heads // 2)
    after_core(1)
    attend_back(1, heads // 2, heads)
    after_y(0)
    if lines > 2:
        kv_wait(2)
    attend_back(2, 0, heads // 2)
    after_y(1)
    attend_back(2, heads // 2, heads)
    for d in range(3, lines):
        kv_wait(d)

    def far(d, carry):
        attend(z - d, False)
        return carry

    lax.fori_loop(3, z + 1, far, 0)

    def write(h, carry):
        at = pl.ds(pl.multiple_of(h * block, block), block)
        o = (acc[at, :] / l_sc[at, :]).astype(BF16)
        for g in range(group):
            attended[:, pl.ds(pl.multiple_of(h * block + g * HD, HD), HD)] = o[g * rows:(g + 1) * rows, :]
        return carry

    lax.fori_loop(0, heads, write, 0)

    for zs in range(lines):
        @pl.when(zs != z)
        def _(zs=zs):
            line_back(0, zs, zs).wait_recv()
            line_back(1, zs, zs).wait_recv()

    col = iota((rows, lines * MAIN), 1)
    owns = chosen == col // (per * MAIN)
    pick_main = onehot(owns & (rank == col % MAIN))
    for k in range(8):
        at = slice(k * pack, (k + 1) * pack)
        pick_ext = onehot(owns & (rank >= MAIN) & ((rank - MAIN) * 8 + k == col % MAIN))
        sums = jnp.dot(pick_main, r3[:, at], preferred_element_type=F32)
        sums += jnp.dot(pick_ext, r3[:, width:], preferred_element_type=F32)
        mixed[:, at] = (states[:, at].astype(F32) + mixing * sums).astype(BF16)

    for i in range(2):
        core_swap(i).wait_send()
        y_swap(i).wait_send()
    for zt in range(lines):
        @pl.when(zt != z)
        def _(zt=zt):
            line_back(0, zt, z).wait_send()
            line_back(1, zt, z).wait_send()
            x_line(zt).wait_send()
    for d in range(lines):
        p = dev((z + d) % lines, y, c)
        x_copy(1, d, p, ymate).wait_send()
        x_copy(2, d, p, cmate).wait_send()
        x_copy(3, d, dev((z + d) % lines, 1 - y, c), cmate).wait_send()

        @pl.when(z >= d)
        def _(d=d):
            kv_copy(1, d, dev(z - d, y, c), ymate).wait_send()
            kv_copy(2, d, dev(z - d, y, c), cmate).wait_send()
            kv_copy(3, d, dev(z - d, 1 - y, c), cmate).wait_send()
        if d:
            @pl.when(z + d < lines)
            def _(d=d):
                kv_line(d).wait_send()


def solution(mesh):
    n = mesh.shape["ctx"]
    lines = n // Q

    def body(states, queries, keys, values, norm_gain, router, routes, w_gate, w_up, w_down):
        rows, width = states.shape
        kvw = keys.shape[1]
        units = w_gate.shape[0]
        qrows = rows * queries.shape[1] // HD
        slots = n * MAIN
        wide = width + width // 8
        vm = pl.BlockSpec(memory_space=pltpu.VMEM)
        hb = pl.BlockSpec(memory_space=pl.ANY)
        dma = pltpu.SemaphoreType.DMA
        return pl.pallas_call(
            functools.partial(kernel, n),
            out_shape=(jax.ShapeDtypeStruct(queries.shape, BF16), jax.ShapeDtypeStruct(states.shape, BF16)),
            in_specs=[vm, vm, hb, hb, vm, vm, vm, hb, hb, hb],
            out_specs=(vm, vm),
            scratch_shapes=[
                pltpu.VMEM((n * rows, 2 * kvw), BF16),
                pltpu.VMEM((slots, wide), BF16),
                pltpu.VMEM((slots + 2 * n, width), BF16),
                pltpu.VMEM((E * MAIN, wide), BF16),
                pltpu.VMEM((slots, wide), BF16),
                pltpu.VMEM((slots + 2 * n, units), BF16),
                pltpu.VMEM((units, width), BF16),
                pltpu.VMEM((units, width), BF16),
                pltpu.VMEM((units, width), BF16),
                pltpu.VMEM((slots // 2, wide), BF16),
                pltpu.VMEM((slots // 4, wide), BF16),
                pltpu.VMEM((lines * MAIN, wide), BF16),
                pltpu.VMEM((qrows, HD), BF16),
                pltpu.VMEM((qrows, HD), F32),
                pltpu.VMEM((qrows, HD), F32),
                pltpu.VMEM((qrows, HD), F32),
                dma((3,)),
                dma((2,)),
                dma((4, lines)),
                dma((n,)),
                dma((4, lines)),
                dma((n,)),
                dma((2, 2)),
                dma((2, 2)),
                dma((2, lines)),
                dma((2, lines)),
            ],
            compiler_params=pltpu.CompilerParams(
                collective_id=0, has_side_effects=True, vmem_limit_bytes=63 * 1024 * 1024),
        )(states, queries, keys, values, norm_gain.reshape(1, width), router.T, routes.T, w_gate, w_up, w_down)

    tokens = P(("groups", "ctx"), None)
    units = P("ctx", None)
    return jax.shard_map(
        body, mesh=mesh,
        in_specs=(tokens, tokens, tokens, tokens, P(), P(), tokens, units, units, units),
        out_specs=(tokens, tokens), check_vma=False)
```

```python
import functools
import math

import jax
import jax.numpy as jnp
from jax import lax
from jax.experimental import pallas as pl
from jax.experimental.pallas import tpu as pltpu
from jax.sharding import PartitionSpec as P

HD = 128
E = 2
CAP = 18
MAIN = 16
Q = 4
MESH = pl.DeviceIdType.MESH
F32 = jnp.float32
BF16 = jnp.bfloat16
NT = (((1,), (1,)), ((), ()))


def iota(shape, dim):
    return lax.broadcasted_iota(jnp.int32, shape, dim)


def onehot(mask):
    return jnp.where(mask, 1.0, 0.0).astype(BF16)


def kernel(n, states, queries, keys, values, gain, router, routes, w_gate, w_up, w_down,
           attended, mixed, kv, x, x2, xb, part, hid, wg, wu, wd, r1, r2, r3, qs, m_sc, l_sc, acc,
           w_sem, loc_sem, kv_send, kv_recv, x_send, x_recv, r_send, r_recv, z_send, z_recv):
    rows, width = states.shape
    lines = n // Q
    per = lines // E
    kvw = keys.shape[1]
    heads = kvw // HD
    group = queries.shape[1] // kvw
    pack = width // 8
    wide = width + pack
    me = lax.axis_index("ctx")
    z = me // Q
    y = (me % Q) // 2
    c = me % 2
    ymate = z * Q + (1 - y) * 2 + c
    cmate = z * Q + y * 2 + (1 - c)

    def dev(zz, yy, cc):
        return zz * Q + yy * 2 + cc

    def slot(p):
        return ((p % 2) * 2 + (p % Q) // 2) * lines + p // Q

    def wcopy(i):
        src = (w_gate, w_up, w_down)[i]
        dst = (wg, wu, wd)[i]
        return pltpu.make_async_copy(src, dst, w_sem.at[i])

    def own_kv(i):
        src = (keys, values)[i]
        return pltpu.make_async_copy(
            src, kv.at[pl.ds(pl.multiple_of(me * rows, rows), rows), pl.ds(i * kvw, kvw)], loc_sem.at[i])

    own_kv(0).start()
    own_kv(1).start()
    for i in range(3):
        wcopy(i).start()

    barrier = pltpu.get_barrier_semaphore()
    for d in range(1, lines):
        pl.semaphore_signal(barrier, inc=1, device_id={"ctx": dev((z + d) % lines, y, c)}, device_id_type=MESH)
    for mate in (ymate, cmate):
        pl.semaphore_signal(barrier, inc=1, device_id={"ctx": mate}, device_id_type=MESH)

    def kv_block(p):
        return kv.at[pl.ds(pl.multiple_of(p * rows, rows), rows)]

    def kv_copy(kind, index, p, to):
        return pltpu.make_async_remote_copy(
            src_ref=kv_block(p), dst_ref=kv_block(p), send_sem=kv_send.at[kind, index], recv_sem=kv_recv.at[p],
            device_id={"ctx": to}, device_id_type=MESH)

    def x_block(p):
        return x.at[pl.ds(pl.multiple_of(slot(p) * MAIN, MAIN), MAIN)]

    def x_copy(kind, index, p, to):
        return pltpu.make_async_remote_copy(
            src_ref=x_block(p), dst_ref=x_block(p), send_sem=x_send.at[kind, index], recv_sem=x_recv.at[p],
            device_id={"ctx": to}, device_id_type=MESH)

    def x_line(zt):
        return pltpu.make_async_remote_copy(
            src_ref=xb.at[pl.ds((zt // per) * MAIN, MAIN)], dst_ref=x_block(me), send_sem=x_send.at[0, zt],
            recv_sem=x_recv.at[me], device_id={"ctx": dev(zt, y, c)}, device_id_type=MESH)

    def kv_line(d):
        return kv_copy(0, d, dev(z - d + 1, y, c), dev(z + 1, y, c))

    def kv_forward(d):
        p = dev(z - d, y, c)

        @pl.when(z >= d)
        def _():
            if d:
                kv_copy(0, d, p, me).wait_recv()
                if d + 1 < lines:
                    @pl.when(z + 1 < lines)
                    def _():
                        kv_line(d + 1).start()
            kv_copy(1, d, p, ymate).start()
            kv_copy(2, d, p, cmate).start()

    def kv_forward_y(d):
        p = dev(z - d, 1 - y, c)

        @pl.when(z >= d)
        def _():
            kv_copy(1, d, p, ymate).wait_recv()
            kv_copy(3, d, p, cmate).start()

    def kv_wait(d):
        @pl.when(z >= d)
        def _():
            kv_copy(2, d, dev(z - d, y, 1 - c), cmate).wait_recv()
            kv_copy(3, d, dev(z - d, 1 - y, 1 - c), cmate).wait_recv()

    own_kv(0).wait()
    own_kv(1).wait()
    pl.semaphore_wait(barrier, lines + 1)
    kv_forward(0)

    st = states[...].astype(F32)
    meansq = jnp.mean(st * st, axis=-1, keepdims=True)
    normed = (st * lax.rsqrt(meansq + 1e-05) * gain[...]).astype(BF16)
    chosen = jnp.transpose(jnp.broadcast_to(routes[...].astype(F32), (HD, rows)))[:, :1].astype(jnp.int32)
    member = chosen == iota((rows, HD), 1)
    before = onehot(iota((rows, rows), 1) < iota((rows, rows), 0))
    ahead = jnp.dot(before, onehot(member), preferred_element_type=F32)
    rank = jnp.sum(jnp.where(member, ahead, 0.0), axis=1, keepdims=True).astype(jnp.int32)
    down_rows = iota((E * MAIN, rows), 0)

    def across(v):
        return jnp.transpose(jnp.broadcast_to(v.astype(F32), (rows, HD)))[: E * MAIN].astype(jnp.int32)

    main_slot = jnp.where((chosen < E) & (rank < MAIN), chosen * MAIN + rank, -1)
    place = onehot(across(main_slot) == down_rows)
    xb[:, :width] = jnp.dot(place, normed, preferred_element_type=F32).astype(BF16)
    ext_slot = jnp.where((chosen < E) & (rank >= MAIN), chosen * MAIN + (rank - MAIN) * 8, -HD)
    ext_slot = across(ext_slot)
    ext = jnp.zeros((E * MAIN, pack), F32)
    for k in range(8):
        sel = onehot(ext_slot + k == down_rows)
        ext += jnp.dot(sel, normed[:, k * pack:(k + 1) * pack], preferred_element_type=F32)
    xb[:, width:] = ext.astype(BF16)
    logits = lax.dot_general(normed, router[...], NT, preferred_element_type=F32)
    picked = jnp.sum(jnp.where(chosen == iota(logits.shape, 1), logits, 0.0), axis=1, keepdims=True)
    mixing = jax.nn.sigmoid(picked)

    x[pl.ds(pl.multiple_of(slot(me) * MAIN, MAIN), MAIN), :] = jnp.where(z < per, xb[:MAIN, :], xb[MAIN:, :])

    for zt in range(lines):
        @pl.when(zt != z)
        def _(zt=zt):
            x_line(zt).start()

    def x_forward(d):
        zs = (z + d) % lines
        p = dev(zs, y, c)
        if d:
            x_copy(0, 0, p, me).wait_recv()
        x_copy(1, d, p, ymate).start()
        x_copy(2, d, p, cmate).start()

    def x_forward_y(d):
        zs = (z + d) % lines
        p = dev(zs, 1 - y, c)
        x_copy(1, d, p, ymate).wait_recv()
        x_copy(3, d, p, cmate).start()

    def x_wait(d):
        zs = (z + d) % lines
        x_copy(2, d, dev(zs, y, 1 - c), cmate).wait_recv()
        x_copy(3, d, dev(zs, 1 - y, 1 - c), cmate).wait_recv()

    x_forward(0)
    if lines > 1:
        @pl.when(z + 1 < lines)
        def _():
            kv_line(1).start()
    for h in range(heads * group):
        qs[h * rows:(h + 1) * rows, :] = queries[:, h * HD:(h + 1) * HD]

    block = group * rows
    span = Q * rows
    scale = math.log2(math.e) / math.sqrt(HD)

    tile = block // 2

    def attend(zs, masked, first=0, last=heads):
        def head(h, carry):
            keys_at = pl.ds(pl.multiple_of(zs * span, span), span)
            k = kv[keys_at, pl.ds(pl.multiple_of(h * HD, HD), HD)]
            v = kv[keys_at, pl.ds(pl.multiple_of(kvw + h * HD, HD), HD)]
            both = jnp.concatenate([v, jnp.ones((span, HD), BF16)], axis=1)
            for low in range(0, block, tile):
                at = pl.ds(pl.multiple_of(h * block + low, tile), tile)
                s = lax.dot_general(qs[at, :], k, NT, preferred_element_type=F32) * scale
                if masked:
                    seen = iota((tile, span), 1) <= (me % Q) * rows + iota((tile, span), 0) % rows
                    s = jnp.where(seen, s, -1e30)
                top = jnp.max(s, axis=-1, keepdims=True)
                if not masked:
                    old = m_sc[at, :1]
                    top = jnp.maximum(old, top)
                e = jnp.exp2(s - top).astype(BF16)
                sums = jnp.dot(e, both, preferred_element_type=F32)
                out, total = sums[:, :HD], sums[:, HD:]
                if not masked:
                    fade = jnp.exp2(old - top)
                    total += fade * l_sc[at, :]
                    out += fade * acc[at, :]
                m_sc[at, :] = jnp.broadcast_to(top, (tile, HD))
                l_sc[at, :] = total
                acc[at, :] = out
            return carry

        lax.fori_loop(first, last, head, 0)

    kv_forward_y(0)
    kv_wait(0)
    attend(z, True, 0, heads // 2)
    for d in range(1, lines):
        x_forward(d)
        x_forward_y(d - 1)
    x_forward_y(lines - 1)
    attend(z, True, heads // 2, heads)
    for d in range(lines):
        x_wait(d)

    slots = n * MAIN
    over = 2 * n

    def unpick(k, shape, s_dim):
        j, i = iota(shape, 1 - s_dim), iota(shape, s_dim)
        return onehot((i // MAIN == j // 2) & (i % MAIN == (j % 2) * 8 + k))

    x2[:slots, :] = x[:, :width]
    for k in range(8):
        x2[slots:, k * pack:(k + 1) * pack] = jnp.dot(
            unpick(k, (over, slots), 1), x[:, width:], preferred_element_type=F32).astype(BF16)

    units = w_gate.shape[0]
    chunk = min(256, units)
    wcopy(0).wait()
    wcopy(1).wait()
    steps = units // chunk

    def gate_up(i, carry):
        at = pl.ds(pl.multiple_of(i * chunk, chunk), chunk)
        g = lax.dot_general(x2[...], wg[at, :], NT, preferred_element_type=F32)
        u = lax.dot_general(x2[...], wu[at, :], NT, preferred_element_type=F32)
        hid[:, at] = (g / (1.0 + jnp.exp(-g)) * u).astype(BF16)
        return carry

    lax.fori_loop(0, steps // 2, gate_up, 0)
    if lines > 1:
        kv_forward(1)
    lax.fori_loop(steps // 2, steps, gate_up, 0)
    if lines > 1:
        kv_forward_y(1)
    if lines > 2:
        kv_forward(2)
    wcopy(2).wait()

    part[:, width:] = jnp.zeros((slots, pack), BF16)

    def down(i, carry):
        at = pl.ds(pl.multiple_of(i * 2 * pack, 2 * pack), 2 * pack)
        o = jnp.dot(hid[...], wd[:, at], preferred_element_type=F32).astype(BF16)
        part[:, at] = o[:slots]
        for k in range(2):
            part[:, width:] += jnp.dot(
                unpick(2 * i + k, (slots, over), 0), o[slots:, k * pack:(k + 1) * pack],
                preferred_element_type=F32).astype(BF16)
        return carry

    half, quart = slots // 2, slots // 4
    sides = ((0, 4 * pack), (4 * pack, wide - 4 * pack))

    def swap(src_at, dst, k, i, to):
        cols = pl.ds(*sides[i])
        return pltpu.make_async_remote_copy(
            src_ref=part.at[src_at, cols], dst_ref=dst.at[:, cols], send_sem=r_send.at[k, i],
            recv_sem=r_recv.at[k, i], device_id={"ctx": to}, device_id_type=MESH)

    def core_swap(i):
        return swap(pl.ds(pl.multiple_of((1 - c) * half, half), half), r1, 0, i, cmate)

    def y_swap(i):
        return swap(pl.ds(pl.multiple_of((c * 2 + 1 - y) * quart, quart), quart), r2, 1, i, ymate)

    def own_rows(zt):
        return pl.ds(pl.multiple_of((c * 2 + y) * quart + zt * MAIN, MAIN), MAIN)

    def line_back(i, zt, at):
        cols = pl.ds(*sides[i])
        return pltpu.make_async_remote_copy(
            src_ref=part.at[own_rows(zt), cols],
            dst_ref=r3.at[pl.ds(pl.multiple_of(at * MAIN, MAIN), MAIN), cols],
            send_sem=z_send.at[i, zt], recv_sem=z_recv.at[i, at], device_id={"ctx": dev(zt, y, c)},
            device_id_type=MESH)

    def add(at, other, i):
        cols = pl.ds(*sides[i])
        part[at, cols] = (part[at, cols].astype(F32) + other[:, cols].astype(F32)).astype(BF16)

    def after_core(i):
        core_swap(i).wait_recv()
        add(pl.ds(pl.multiple_of(c * half, half), half), r1, i)
        y_swap(i).start()

    def after_y(i):
        y_swap(i).wait_recv()
        add(pl.ds(pl.multiple_of((c * 2 + y) * quart, quart), quart), r2, i)
        cols = pl.ds(*sides[i])
        for zt in range(lines):
            @pl.when(zt != z)
            def _(zt=zt):
                line_back(i, zt, z).start()

            @pl.when(zt == z)
            def _(zt=zt):
                r3[zt * MAIN:(zt + 1) * MAIN, cols] = part[own_rows(zt), cols]

    def attend_back(d, first, last):
        if d < lines:
            @pl.when(z >= d)
            def _():
                attend(z - d, False, first, last)

    lax.fori_loop(0, 2, down, 0)
    core_swap(0).start()
    lax.fori_loop(2, 4, down, 0)
    core_swap(1).start()
    for d in range(3, lines):
        kv_forward(d)
    for d in range(2, lines):
        kv_forward_y(d)
    after_core(0)
    if lines > 1:
        kv_wait(1)
    attend_back(1, 0, heads // 2)
    after_core(1)
    attend_back(1, heads // 2, heads)
    after_y(0)
    if lines > 2:
        kv_wait(2)
    attend_back(2, 0, heads // 2)
    after_y(1)
    attend_back(2, heads // 2, heads)
    for d in range(3, lines):
        kv_wait(d)

    def far(d, carry):
        attend(z - d, False)
        return carry

    lax.fori_loop(3, z + 1, far, 0)

    def write(h, carry):
        at = pl.ds(pl.multiple_of(h * block, block), block)
        o = (acc[at, :] / l_sc[at, :]).astype(BF16)
        for g in range(group):
            attended[:, pl.ds(pl.multiple_of(h * block + g * HD, HD), HD)] = o[g * rows:(g + 1) * rows, :]
        return carry

    lax.fori_loop(0, heads, write, 0)

    for zs in range(lines):
        @pl.when(zs != z)
        def _(zs=zs):
            line_back(0, zs, zs).wait_recv()
            line_back(1, zs, zs).wait_recv()

    col = iota((rows, lines * MAIN), 1)
    owns = chosen == col // (per * MAIN)
    pick_main = onehot(owns & (rank == col % MAIN))
    for k in range(8):
        at = slice(k * pack, (k + 1) * pack)
        pick_ext = onehot(owns & (rank >= MAIN) & ((rank - MAIN) * 8 + k == col % MAIN))
        sums = jnp.dot(pick_main, r3[:, at], preferred_element_type=F32)
        sums += jnp.dot(pick_ext, r3[:, width:], preferred_element_type=F32)
        mixed[:, at] = (states[:, at].astype(F32) + mixing * sums).astype(BF16)

    for i in range(2):
        core_swap(i).wait_send()
        y_swap(i).wait_send()
    for zt in range(lines):
        @pl.when(zt != z)
        def _(zt=zt):
            line_back(0, zt, z).wait_send()
            line_back(1, zt, z).wait_send()
            x_line(zt).wait_send()
    for d in range(lines):
        p = dev((z + d) % lines, y, c)
        x_copy(1, d, p, ymate).wait_send()
        x_copy(2, d, p, cmate).wait_send()
        x_copy(3, d, dev((z + d) % lines, 1 - y, c), cmate).wait_send()

        @pl.when(z >= d)
        def _(d=d):
            kv_copy(1, d, dev(z - d, y, c), ymate).wait_send()
            kv_copy(2, d, dev(z - d, y, c), cmate).wait_send()
            kv_copy(3, d, dev(z - d, 1 - y, c), cmate).wait_send()
        if d:
            @pl.when((z >= d - 1) & (z + 1 < lines))
            def _(d=d):
                kv_line(d).wait_send()


def solution(mesh):
    n = mesh.shape["ctx"]
    lines = n // Q

    def body(states, queries, keys, values, norm_gain, router, routes, w_gate, w_up, w_down):
        rows, width = states.shape
        kvw = keys.shape[1]
        units = w_gate.shape[0]
        qrows = rows * queries.shape[1] // HD
        slots = n * MAIN
        wide = width + width // 8
        vm = pl.BlockSpec(memory_space=pltpu.VMEM)
        hb = pl.BlockSpec(memory_space=pl.ANY)
        dma = pltpu.SemaphoreType.DMA
        return pl.pallas_call(
            functools.partial(kernel, n),
            out_shape=(jax.ShapeDtypeStruct(queries.shape, BF16), jax.ShapeDtypeStruct(states.shape, BF16)),
            in_specs=[vm, vm, hb, hb, vm, vm, vm, hb, hb, hb],
            out_specs=(vm, vm),
            scratch_shapes=[
                pltpu.VMEM((n * rows, 2 * kvw), BF16),
                pltpu.VMEM((slots, wide), BF16),
                pltpu.VMEM((slots + 2 * n, width), BF16),
                pltpu.VMEM((E * MAIN, wide), BF16),
                pltpu.VMEM((slots, wide), BF16),
                pltpu.VMEM((slots + 2 * n, units), BF16),
                pltpu.VMEM((units, width), BF16),
                pltpu.VMEM((units, width), BF16),
                pltpu.VMEM((units, width), BF16),
                pltpu.VMEM((slots // 2, wide), BF16),
                pltpu.VMEM((slots // 4, wide), BF16),
                pltpu.VMEM((lines * MAIN, wide), BF16),
                pltpu.VMEM((qrows, HD), BF16),
                pltpu.VMEM((qrows, HD), F32),
                pltpu.VMEM((qrows, HD), F32),
                pltpu.VMEM((qrows, HD), F32),
                dma((3,)),
                dma((2,)),
                dma((4, lines)),
                dma((n,)),
                dma((4, lines)),
                dma((n,)),
                dma((2, 2)),
                dma((2, 2)),
                dma((2, lines)),
                dma((2, lines)),
            ],
            compiler_params=pltpu.CompilerParams(
                collective_id=0, has_side_effects=True, vmem_limit_bytes=63 * 1024 * 1024),
        )(states, queries, keys, values, norm_gain.reshape(1, width), router.T, routes.T, w_gate, w_up, w_down)

    tokens = P(("groups", "ctx"), None)
    units = P("ctx", None)
    return jax.shard_map(
        body, mesh=mesh,
        in_specs=(tokens, tokens, tokens, tokens, P(), P(), tokens, units, units, units),
        out_specs=(tokens, tokens), check_vma=False)
```
